256 devices in a mesh: task: 4 (over x_lo, core), row: 8 (over y, x_hi), col: 8 (over z).
Axes of the slice: x: 4 (x_hi: 2, x_lo: 2; x = x_hi * 2 + x_lo), y: 4, z: 8, core: 2. Of those that a mesh axis runs over, the one named last changes fastest.
Arguments:
- acts: bfloat16 [4, 6, 512, 14336], P('task', None, 'col', 'row'), may hold values from -6 to 6
- grads: bfloat16 [4, 6, 512, 8192], P('task', None, 'row', 'col'), may hold values from -0.29882812 to 0.29882812
- weights: bfloat16 [4, 14336, 8192], P('task', 'row', 'col'), may hold values from -6 to 6
Outputs:
- merged: bfloat16 [14336, 8192], P('row', 'col')
The draws below stay inside these ranges and needn't reach their ends.
All inputs are finite; a program needn't handle non-finite values.
Results may differ from the reference program's by a relative error of at most 0.001.
Values may be sent and summed in bfloat16 or wider, within the bound.
No kernel may reach another device: no remote copies, remote signals or barrier semaphores. Data moves between devices by JAX's collectives and lax.ppermute only.
A program may use at most 128 MiB of HBM per device.

```python
import jax
import jax.numpy as jnp
from jax import lax

FFI = 14336
D = 8192
TOK = 512
SAMPLES = 6
TASKS = 4


def levels(own_key, extent, split, low, largest):
    gain, own = 1.0, jax.random.fold_in(own_key, 6)
    for axis_at, parts in split:
        draws = jnp.exp(jax.random.uniform(jax.random.fold_in(own, axis_at), (parts,), jnp.float32, low / len(split), largest / len(split)))
        gain = gain * jnp.repeat(draws, extent[axis_at] // parts).reshape([-1 if axis == axis_at else 1 for axis in range(len(extent))])
    return gain


def normal_values(stream_key, dims, spread, most, pieces=(), kind=jnp.bfloat16):
    factor_of = levels(stream_key, dims, pieces, -0.22, 0.18) if pieces else 1.0
    entries = jax.random.normal(stream_key, dims, jnp.float32) * spread * factor_of
    return jnp.minimum(jnp.maximum(entries, -most), most).astype(kind)


def setup_inputs(seed: int = 0) -> dict:
    streams_of = jax.random.split(jax.random.key(seed), 4)
    acts = normal_values(streams_of[0], (TASKS, SAMPLES, TOK, FFI), 1.0, 6.0, ((0, 4), (2, 8), (3, 8)))
    grads = normal_values(streams_of[1], (TASKS, SAMPLES, TOK, D), 0.05, 0.29882812, ((0, 4), (2, 8), (3, 8)))
    weights = normal_values(streams_of[2], (TASKS, FFI, D), 1.0, 6.0, ((0, 4), (1, 8), (2, 8)))
    return dict(acts=acts, grads=grads, weights=weights)


EPS = 1e-6


def reference(acts, grads, weights):
    numerator = jnp.zeros((FFI, D), jnp.float32)
    denominator = jnp.zeros((FFI, D), jnp.float32)
    for task_id in range(TASKS):
        def add_sample(fisher, sample_id):
            left = acts[task_id, sample_id]
            right = grads[task_id, sample_id]
            sample_grad = lax.dot_general(left, right, (((0,), (0,)), ((), ())), preferred_element_type=jnp.float32)
            return fisher + sample_grad * sample_grad, None

        fisher, unused = lax.scan(add_sample, jnp.zeros((FFI, D), jnp.float32), jnp.arange(SAMPLES))
        numerator = numerator + fisher * weights[task_id].astype(jnp.float32)
        denominator = denominator + fisher
    return (numerator / (denominator + EPS)).astype(jnp.bfloat16)
```

```python
import functools

import jax
import jax.numpy as jnp
from jax import lax
from jax.experimental import pallas as pl
from jax.experimental.pallas import tpu as pltpu
from jax.sharding import PartitionSpec as P

EPS = 1e-06
F32, BF16 = jnp.float32, jnp.bfloat16
ANY = pl.BlockSpec(memory_space=pl.ANY)
LIMIT = pltpu.CompilerParams(vmem_limit_bytes=56 * 2**20)


def place():
    task, row = lax.axis_index("task"), lax.axis_index("row")
    return task // 2, task % 2, row // 2, row % 2


def plane(x, dy, hi, lo):
    perm = [
        (t * 8 + 2 * y + h, (t ^ (2 * lo)) * 8 + 2 * ((y + dy) % 4) + (h ^ hi))
        for t in range(4)
        for y in range(4)
        for h in range(2)
    ]
    return lax.ppermute(x, ("task", "row"), perm)


def pair(x):
    return lax.ppermute(x, "task", [(t, t ^ 2) for t in range(4)])


def core(x):
    return lax.ppermute(x, "task", [(t, t ^ 1) for t in range(4)])


def block_of(meta):
    back, flip = meta
    _, _, y, hi = place()
    return 2 * ((y + 4 - back) % 4) + (hi ^ flip if flip else hi)


def fetch(metas, acts, pieces, a, g, sems):
    tok = pieces[0].shape[1]

    def copies(s):
        out = [pltpu.make_async_copy(acts.at[s], a.at[s], sems.at[s])]
        for meta, piece in zip(metas, pieces):
            rows = pl.ds(pl.multiple_of(tok * block_of(meta), tok), tok)
            out.append(pltpu.make_async_copy(piece.at[s], g.at[s, rows], sems.at[s]))
        return out

    return copies


def square_sum(copies, count, a, g, f):
    def step(s, _):
        for c in copies(s):
            c.wait()
        d = lax.dot_general(
            a[s], g[s], (((0,), (0,)), ((), ())), preferred_element_type=F32
        )
        f[...] = jnp.where(s == 0, 0.0, f[...]) + d * d
        return 0

    lax.fori_loop(0, count, step, 0)


def first_kernel(metas, acts, *refs):
    n = len(metas)
    pieces, (out, a, g, f, sems, osem) = refs[:n], refs[n:]
    copies = fetch(metas, acts, pieces, a, g, sems)
    count = a.shape[0]
    for s in range(count):
        for c in copies(s):
            c.start()
    square_sum(copies, count, a, g, f)
    cp = pltpu.make_async_copy(f, out, osem)
    cp.start()
    cp.wait()


def second_kernel(metas, acts, *refs):
    n = len(metas)
    pieces = refs[:n]
    f1_hbm, w1_hbm, w2_hbm, keep, send, a, g, f, f1, w1, w2, sems, xsem, osem = refs[n:]
    copies = fetch(metas, acts, pieces, a, g, sems)
    count = a.shape[0]
    lo, me, _, _ = place()
    rows = f.shape[0]
    half = rows // 2
    own = pl.ds(pl.multiple_of(lo * rows, 16), rows)
    extra = [
        pltpu.make_async_copy(f1_hbm, f1, xsem.at[0]),
        pltpu.make_async_copy(w1_hbm.at[0, own], w1, xsem.at[1]),
        pltpu.make_async_copy(w2_hbm, w2, xsem.at[2]),
    ]
    for s in range(count):
        for c in copies(s):
            c.start()
        if s == 0:
            for c in extra:
                c.start()
    square_sum(copies, count, a, g, f)
    for c in extra:
        c.wait()
    one, two = f1[...], f[...]
    f1[...] = one * w1[...].astype(F32) + two * w2[...].astype(F32)
    f[...] = one + two
    outs = []
    for i, src in enumerate((f1, f)):
        for j, (dst, which) in enumerate(((send, 1 - me), (keep, me))):
            at = pl.ds(pl.multiple_of(which * half, 16), half)
            outs.append(pltpu.make_async_copy(src.at[at], dst.at[i], osem.at[2 * i + j]))
    for c in outs:
        c.start()
    for c in outs:
        c.wait()


def share_kernel(keep, got, out):
    den = keep[1] + got[1]
    out[...] = ((keep[0] + got[0]) / (den + EPS)).astype(BF16)


def gather_kernel(own, by_core, by_pair, by_both, out, held, sems, osems):
    lo, me, _, _ = place()
    n = own.shape[0]
    ins, outs = [], []
    for i, (src, l, c) in enumerate(
        ((own, lo, me), (by_core, lo, 1 - me), (by_pair, 1 - lo, me), (by_both, 1 - lo, 1 - me))
    ):
        at = pl.ds(pl.multiple_of((2 * l + c) * n, 16), n)
        ins.append(pltpu.make_async_copy(src, held.at[i], sems.at[i]))
        outs.append(pltpu.make_async_copy(held.at[i], out.at[at], osems.at[i]))
    for c in ins:
        c.start()
    for i, o in zip(ins, outs):
        i.wait()
        o.start()
    for c in outs:
        c.wait()


def body(acts, grads, weights):
    _, count, tok, rows = acts.shape
    cols = grads.shape[3]
    half = rows // 2
    lo = lax.axis_index("task") // 2
    g0 = grads[0]

    def part(x, which, axis):
        return lax.dynamic_slice_in_dim(x, which * half, half, axis)

    own_acts = part(acts[0], lo, 2)
    a1 = lax.all_gather(own_acts, "col", axis=1, tiled=True)
    gd = plane(g0, 0, 0, 1)
    g0n, g0p = plane(g0, 1, 0, 0), plane(g0, -1, 0, 0)
    gx = plane(g0, 0, 1, 1)
    other_acts = pair(part(acts[0], 1 - lo, 2))
    a2 = lax.all_gather(other_acts, "col", axis=1, tiled=True)
    go = plane(gd, 0, 1, 1)
    g02 = plane(g0n, 1, 0, 0)
    gon, gop = plane(go, 1, 0, 0), plane(go, -1, 0, 0)
    go2 = plane(gop, -1, 0, 0)
    gxn, gxp, gx2 = plane(g0n, 0, 1, 1), plane(g0p, 0, 1, 1), plane(g02, 0, 1, 1)
    gdn, gdp = plane(gd, 1, 0, 0), plane(gd, -1, 0, 0)
    gd2 = plane(gdn, 1, 0, 0)
    w2 = pair(part(weights[0], 1 - lo, 0))

    metas1 = [(0, 0), (1, 0), (3, 0), (2, 0), (0, 1), (1, 1), (3, 1), (2, 1)]
    pieces1 = (g0, g0n, g0p, g02, go, gon, gop, go2)
    pieces2 = (gd, gdn, gdp, gd2, gx, gxn, gxp, gx2)
    total = tok * 8
    common = [
        pltpu.VMEM((count, total, half), BF16),
        pltpu.VMEM((count, total, cols), BF16),
        pltpu.VMEM((half, cols), F32),
    ]
    flops = 2 * count * total * half * cols
    cost = pl.CostEstimate(flops=flops, bytes_accessed=16 * 2**20, transcendentals=0)
    f1 = pl.pallas_call(
        functools.partial(first_kernel, metas1),
        out_shape=jax.ShapeDtypeStruct((half, cols), F32),
        in_specs=[ANY] * 9,
        out_specs=ANY,
        scratch_shapes=common
        + [pltpu.SemaphoreType.DMA((count,)), pltpu.SemaphoreType.DMA],
        compiler_params=LIMIT,
        cost_estimate=cost,
        name="own_task",
    )(a1, *pieces1)
    quarter = half // 2
    two = jax.ShapeDtypeStruct((2, quarter, cols), F32)
    keep, send = pl.pallas_call(
        functools.partial(second_kernel, metas1),
        out_shape=(two, two),
        in_specs=[ANY] * 12,
        out_specs=(ANY, ANY),
        scratch_shapes=common
        + [
            pltpu.VMEM((half, cols), F32),
            pltpu.VMEM((half, cols), BF16),
            pltpu.VMEM((half, cols), BF16),
            pltpu.SemaphoreType.DMA((count,)),
            pltpu.SemaphoreType.DMA((3,)),
            pltpu.SemaphoreType.DMA((4,)),
        ],
        compiler_params=LIMIT,
        cost_estimate=cost,
        name="other_task",
    )(a2, *pieces2, f1, weights, w2)
    got = core(send)
    steps = 4
    q = pl.pallas_call(
        share_kernel,
        grid=(steps,),
        out_shape=jax.ShapeDtypeStruct((quarter, cols), BF16),
        in_specs=[pl.BlockSpec((2, quarter // steps, cols), lambda i: (0, i, 0))] * 2,
        out_specs=pl.BlockSpec((quarter // steps, cols), lambda i: (i, 0)),
        compiler_params=LIMIT,
        name="share",
    )(keep, got)
    by_pair = pair(q)
    by_core = core(q)
    by_both = core(by_pair)
    return pl.pallas_call(
        gather_kernel,
        out_shape=jax.ShapeDtypeStruct((rows, cols), BF16),
        in_specs=[ANY] * 4,
        out_specs=ANY,
        scratch_shapes=[
            pltpu.VMEM((4, quarter, cols), BF16),
            pltpu.SemaphoreType.DMA((4,)),
            pltpu.SemaphoreType.DMA((4,)),
        ],
        compiler_params=LIMIT,
        name="whole",
    )(q, by_core, by_pair, by_both)


def solution(mesh):
    placed = (P("task", None, "col", "row"), P("task", None, "row", "col"), P("task", "row", "col"))
    return jax.shard_map(
        body, mesh=mesh, in_specs=placed, out_specs=P("row", "col"), check_vma=False
    )
```

```python
import functools

import jax
import jax.numpy as jnp
from jax import lax
from jax.experimental import pallas as pl
from jax.experimental.pallas import tpu as pltpu
from jax.sharding import PartitionSpec as P

EPS = 1e-06
F32, BF16 = jnp.float32, jnp.bfloat16
ANY = pl.BlockSpec(memory_space=pl.ANY)
LIMIT = pltpu.CompilerParams(vmem_limit_bytes=56 * 2**20)
CHUNKS = (512, 384)


ORDER = (
    "o,o,0",
    "t,give,0",
    "g,g,0",
    "x,g,0",
    "o,o,1",
    "t,t,0",
    "d,g,0<t0",
    "g,g,1",
    "x,g,1",
    "o,o,2",
    "t,t,1",
    "u,d,0",
    "g,g,2",
    "d,d,0",
    "o,o,3",
    "t,t,2",
    "w,wgive,0",
    "d,d,1",
    "u,u,0",
    "x,g,2",
    "o,o,4",
    "t,t,3<x0<g3",
    "d,d,2",
    "u,u,1",
    "x,g,3",
    "o,o,5",
    "t,t,4",
    "u,u,2",
    "o,o,6",
    "t,t,5<d3<x1",
    "t,t,6<u3<x2",
)


def place():
    task, row = lax.axis_index("task"), lax.axis_index("row")
    return task // 2, task % 2, row // 2, row % 2


def ring_y(x):
    perm = [
        (t * 8 + 2 * y + h, t * 8 + 2 * ((y + 1 - 2 * (t % 2)) % 4) + h)
        for t in range(4)
        for y in range(4)
        for h in range(2)
    ]
    return lax.ppermute(x, ("task", "row"), perm)


def ring_z(x):
    perm = [(t * 8 + z, t * 8 + (z + 1 - 2 * (t % 2)) % 8) for t in range(4) for z in range(8)]
    return lax.ppermute(x, ("task", "col"), perm)


def cross(x):
    perm = [(t * 8 + r, (t ^ 2) * 8 + (r ^ 1)) for t in range(4) for r in range(8)]
    return lax.ppermute(x, ("task", "row"), perm)


def pair(x):
    return lax.ppermute(x, "task", [(t, t ^ 2) for t in range(4)])


def core(x):
    return lax.ppermute(x, "task", [(t, t ^ 1) for t in range(4)])


def grad_block(back, flip):
    _, me, y, hi = place()
    return 2 * ((y + 4 + (2 * me - 1) * back) % 4) + (hi ^ flip if flip else hi)


def act_block(back):
    return (lax.axis_index("col") + 8 + (2 * lax.rem(lax.axis_index("task"), 2) - 1) * back) % 8


def fetch(first, grad_from, acts, grads, a, g, sems):
    count, tok, size = a.shape[0], a.shape[1] // 8, a.shape[2]

    def begin():
        for s in range(count):
            for back, piece in enumerate(acts):
                rows = pl.ds(pl.multiple_of(tok * act_block(back), tok), tok)
                src = piece.at[s, :, pl.ds(first, size)]
                pltpu.make_async_copy(src, a.at[s, rows], sems.at[s]).start()
            for meta, piece in zip(grad_from, grads):
                rows = pl.ds(pl.multiple_of(tok * grad_block(*meta), tok), tok)
                pltpu.make_async_copy(piece.at[s], g.at[s, rows], sems.at[s]).start()

    def arrive(s):
        pltpu.make_async_copy(a.at[s], a.at[s], sems.at[s]).wait()
        pltpu.make_async_copy(g.at[s], g.at[s], sems.at[s]).wait()

    return begin, arrive


def square_sum(arrive, count, a, g, f):
    def step(s, _):
        arrive(s)
        d = lax.dot_general(
            a[s], g[s], (((0,), (0,)), ((), ())), preferred_element_type=F32
        )
        f[...] = jnp.where(s == 0, 0.0, f[...]) + d * d
        return 0

    lax.fori_loop(0, count, step, 0)


def first_kernel(n, grad_from, *refs):
    m = len(grad_from)
    acts, grads, (out, a, g, f, sems, osem) = refs[:n], refs[n : n + m], refs[n + m :]
    begin, arrive = fetch(0, grad_from, acts, grads, a, g, sems)
    begin()
    square_sum(arrive, a.shape[0], a, g, f)
    cp = pltpu.make_async_copy(f, out, osem)
    cp.start()
    cp.wait()


def second_kernel(n, grad_from, first, rows, *refs):
    m = len(grad_from)
    acts, grads = refs[:n], refs[n : n + m]
    f1_hbm, w1_hbm, w2_hbm, keep, send, a, g, f, f1, w1, w2, sems, xsem, osem = refs[n + m :]
    begin, arrive = fetch(first, grad_from, acts, grads, a, g, sems)
    count, size = a.shape[0], f.shape[0]
    lo, me, _, _ = place()
    half = size // 2
    own = pl.ds(pl.multiple_of(lo * rows + first, 16), size)
    extra = [
        pltpu.make_async_copy(f1_hbm.at[pl.ds(first, size)], f1, xsem.at[0]),
        pltpu.make_async_copy(w1_hbm.at[0, own], w1, xsem.at[1]),
        pltpu.make_async_copy(w2_hbm.at[pl.ds(first, size)], w2, xsem.at[2]),
    ]
    begin()
    for c in extra:
        c.start()
    square_sum(arrive, count, a, g, f)
    for c in extra:
        c.wait()
    one, two = f1[...], f[...]
    f1[...] = one * w1[...].astype(F32) + two * w2[...].astype(F32)
    f[...] = one + two
    outs = []
    for i, src in enumerate((f1, f)):
        for j, (dst, which) in enumerate(((send, 1 - me), (keep, me))):
            at = pl.ds(pl.multiple_of(which * half, 16), half)
            outs.append(pltpu.make_async_copy(src.at[at], dst.at[i], osem.at[2 * i + j]))
    for c in outs:
        c.start()
    for c in outs:
        c.wait()


def share_kernel(keep, got, out):
    den = keep[1] + got[1]
    out[...] = ((keep[0] + got[0]) / (den + EPS)).astype(BF16)


def whole_kernel(first, rows, *refs):
    own, by_core, by_pair, by_both, out, held, sems, osems = refs[-8:]
    lo, me, _, _ = place()
    n = own.shape[0]
    ins, outs = [], []
    for i, (src, l, c) in enumerate(
        ((own, lo, me), (by_core, lo, 1 - me), (by_pair, 1 - lo, me), (by_both, 1 - lo, 1 - me))
    ):
        at = pl.ds(pl.multiple_of(l * rows + first + c * n, 16), n)
        ins.append(pltpu.make_async_copy(src, held.at[i], sems.at[i]))
        outs.append(pltpu.make_async_copy(held.at[i], out.at[at], osems.at[i]))
    for c in ins:
        c.start()
    for i, o in zip(ins, outs):
        i.wait()
        o.start()
    for c in outs:
        c.wait()


def cost(flops, moved):
    return pl.CostEstimate(flops=flops, bytes_accessed=moved, transcendentals=0)


def body(acts, grads, weights):
    _, count, tok, rows = acts.shape
    cols = grads.shape[3]
    half = rows // 2
    total = tok * 8
    lo = lax.axis_index("task") // 2
    have = {"g": [grads[0]]}

    def part(x, which, axis):
        return lax.dynamic_slice_in_dim(x, which * half, half, axis)

    def run(name, move, source, *after):
        x = have[source[0]][source[1]]
        if after:
            x = lax.optimization_barrier((x, *[have[n][i] for n, i in after]))[0]
        have.setdefault(name, []).append(move(x))

    have["o"] = [part(acts[0], lo, 2)]
    have["give"] = [part(acts[0], 1 - lo, 2)]
    have["wgive"] = [part(weights[0], 1 - lo, 0)]
    for line in ORDER:
        name, source, at, *after = line.replace("<", ",").split(",")
        move = {"o": ring_z, "t": ring_z, "g": ring_y, "d": ring_y, "u": ring_y}.get(name, pair)
        if name == "x" or line.startswith("u,d"):
            move = cross
        if line.startswith(("t,give", "d,g")):
            move = pair
        run(name, move, (source, int(at)), *[(x[0], int(x[1:])) for x in after])

    grad_from = [(k, flip) for flip in (0, 1) for k in range(4)]
    sems = pltpu.SemaphoreType.DMA((count,))
    arrays = [*have["o"], *have["g"], *have["u"]]
    f1 = pl.pallas_call(
        functools.partial(first_kernel, 8, grad_from),
        out_shape=jax.ShapeDtypeStruct((half, cols), F32),
        in_specs=[ANY] * len(arrays),
        out_specs=ANY,
        scratch_shapes=[
            pltpu.VMEM((count, total, half), BF16),
            pltpu.VMEM((count, total, cols), BF16),
            pltpu.VMEM((half, cols), F32),
            sems,
            pltpu.SemaphoreType.DMA,
        ],
        compiler_params=LIMIT,
        cost_estimate=cost(2 * count * total * half * cols, 12 * 2**20),
        name="own_task",
    )(*arrays)
    arrays = [*have["t"], *have["d"], *have["x"], f1, weights, *have["w"]]
    out, first = None, 0
    for size in CHUNKS:
        mine = size // 2
        two = jax.ShapeDtypeStruct((2, mine, cols), F32)
        keep, send = pl.pallas_call(
            functools.partial(second_kernel, 8, grad_from, first, half),
            out_shape=(two, two),
            in_specs=[ANY] * len(arrays),
            out_specs=(ANY, ANY),
            scratch_shapes=[
                pltpu.VMEM((count, total, size), BF16),
                pltpu.VMEM((count, total, cols), BF16),
                pltpu.VMEM((size, cols), F32),
                pltpu.VMEM((size, cols), F32),
                pltpu.VMEM((size, cols), BF16),
                pltpu.VMEM((size, cols), BF16),
                sems,
                pltpu.SemaphoreType.DMA((3,)),
                pltpu.SemaphoreType.DMA((4,)),
            ],
            compiler_params=LIMIT,
            cost_estimate=cost(2 * count * total * size * cols, 12 * 2**20),
            name="other_task",
        )(*arrays)
        got = core(send)
        q = pl.pallas_call(
            share_kernel,
            out_shape=jax.ShapeDtypeStruct((mine, cols), BF16),
            compiler_params=LIMIT,
            name="share",
        )(keep, got)
        by_pair = pair(q)
        by_core = core(q)
        by_both = core(by_pair)
        args = (q, by_core, by_pair, by_both)
        args = args if out is None else (out, *args)
        out = pl.pallas_call(
            functools.partial(whole_kernel, first, half),
            out_shape=jax.ShapeDtypeStruct((rows, cols), BF16),
            in_specs=[ANY] * len(args),
            out_specs=ANY,
            scratch_shapes=[
                pltpu.VMEM((4, mine, cols), BF16),
                pltpu.SemaphoreType.DMA((4,)),
                pltpu.SemaphoreType.DMA((4,)),
            ],
            input_output_aliases={} if out is None else {0: 0},
            compiler_params=LIMIT,
            name="whole",
        )(*args)
        first += size
    return out


def solution(mesh):
    placed = (P("task", None, "col", "row"), P("task", None, "row", "col"), P("task", "row", "col"))
    return jax.shard_map(
        body, mesh=mesh, in_specs=placed, out_specs=P("row", "col"), check_vma=False
    )
```

```python
import functools

import jax
import jax.numpy as jnp
from jax import lax
from jax.experimental import pallas as pl
from jax.experimental.pallas import tpu as pltpu
from jax.sharding import PartitionSpec as P

EPS = 1e-06
F32, BF16 = jnp.float32, jnp.bfloat16
HBM = pl.BlockSpec(memory_space=pltpu.HBM)
NEAR = pl.BlockSpec(memory_space=pltpu.VMEM)
LIMIT = pltpu.CompilerParams(vmem_limit_bytes=42 * 2**20)
LITTLE = pltpu.CompilerParams(vmem_limit_bytes=16 * 2**20)
PIECES = (896,)
CHUNKS = (192, 256)


ORDER = (
    "o,o,0",
    "t,give,0",
    "g,g,0",
    "x,g,0",
    "o,o,1",
    "t,t,0",
    "d,g,0",
    "w,wgive,0",
    "g,g,1",
    "x,g,1",
    "o,o,2",
    "t,t,1",
    "u,d,0",
    "g,g,2",
    "d,d,0",
    "o,o,3",
    "t,t,2",
    "d,d,1",
    "u,u,0",
    "x,g,2<t1<w0",
    "o,o,4<d2",
    "t,t,3<x0<g3",
    "d,d,2",
    "u,u,1",
    "x,g,3",
    "o,o,5",
    "t,t,4",
    "u,u,2",
    "o,o,6",
    "t,t,5<x1",
    "t,t,6<x2",
)


def near(x):
    return pltpu.with_memory_space_constraint(x, pltpu.VMEM)


def far(x):
    return pltpu.with_memory_space_constraint(x, pltpu.HBM)


def place():
    task, row = lax.axis_index("task"), lax.axis_index("row")
    return task // 2, task % 2, row // 2, row % 2


def ring_y(x):
    perm = [
        (t * 8 + 2 * y + h, t * 8 + 2 * ((y + 1 - 2 * (t % 2)) % 4) + h)
        for t in range(4)
        for y in range(4)
        for h in range(2)
    ]
    return lax.ppermute(x, ("task", "row"), perm)


def ring_z(x):
    perm = [(t * 8 + z, t * 8 + (z + 1 - 2 * (t % 2)) % 8) for t in range(4) for z in range(8)]
    return lax.ppermute(x, ("task", "col"), perm)


def cross(x):
    perm = [(t * 8 + r, (t ^ 2) * 8 + (r ^ 1)) for t in range(4) for r in range(8)]
    return lax.ppermute(x, ("task", "row"), perm)


def pair(x):
    return lax.ppermute(x, "task", [(t, t ^ 2) for t in range(4)])


def core(x):
    return lax.ppermute(x, "task", [(t, t ^ 1) for t in range(4)])


def grad_block(back, flip):
    _, me, y, hi = place()
    return 2 * ((y + 4 + (2 * me - 1) * back) % 4) + (hi ^ flip if flip else hi)


def act_block(back):
    return (lax.axis_index("col") + 8 + (2 * lax.rem(lax.axis_index("task"), 2) - 1) * back) % 8


def fetch(grad_from, acts, grads, a, g, sems):
    count, tok = a.shape[0], a.shape[1] // 8

    def begin():
        for s in range(count):
            for back, piece in enumerate(acts):
                rows = pl.ds(pl.multiple_of(tok * act_block(back), tok), tok)
                pltpu.make_async_copy(piece.at[s], a.at[s, rows], sems.at[s]).start()
            for meta, piece in zip(grad_from, grads):
                rows = pl.ds(pl.multiple_of(tok * grad_block(*meta), tok), tok)
                pltpu.make_async_copy(piece.at[s], g.at[s, rows], sems.at[s]).start()

    def arrive(s):
        pltpu.make_async_copy(a.at[s], a.at[s], sems.at[s]).wait()
        pltpu.make_async_copy(g.at[s], g.at[s], sems.at[s]).wait()

    return begin, arrive


def square_sum(arrive, count, a, g, f):
    def step(s, _):
        arrive(s)
        d = lax.dot_general(
            a[s], g[s], (((0,), (0,)), ((), ())), preferred_element_type=F32
        )
        f[...] = jnp.where(s == 0, 0.0, f[...]) + d * d
        return 0

    lax.fori_loop(0, count, step, 0)


def first_kernel(n, grad_from, *refs):
    m = len(grad_from)
    acts, grads, (out, a, g, f, sems, osem) = refs[:n], refs[n : n + m], refs[n + m :]
    begin, arrive = fetch(grad_from, acts, grads, a, g, sems)
    begin()
    square_sum(arrive, a.shape[0], a, g, f)
    cp = pltpu.make_async_copy(f, out, osem)
    cp.start()
    cp.wait()


def second_kernel(n, grad_from, *refs):
    m = len(grad_from)
    acts, grads = refs[:n], refs[n : n + m]
    f1_hbm, w1_hbm, *w2_hbm = refs[n + m : n + m + 2 + len(PIECES)]
    keep, *sends, a, g, f, f1, w1, w2, sems, xsem = refs[n + m + 2 + len(PIECES) :]
    begin, arrive = fetch(grad_from, acts, grads, a, g, sems)
    count, size = a.shape[0], f.shape[0]
    lo, me, _, _ = place()
    half = size // 2
    own = pl.ds(pl.multiple_of(lo * size, 16), size)
    extra = [
        pltpu.make_async_copy(f1_hbm, f1, xsem.at[0]),
        pltpu.make_async_copy(w1_hbm.at[0, own], w1, xsem.at[1]),
    ]
    first = 0
    for i, piece in enumerate(w2_hbm):
        at = pl.ds(first, piece.shape[0])
        extra.append(pltpu.make_async_copy(piece, w2.at[at], xsem.at[2 + i]))
        first += piece.shape[0]
    begin()
    for c in extra:
        c.start()
    square_sum(arrive, count, a, g, f)
    for c in extra:
        c.wait()

    def write(out, which, first):
        at = pl.ds(pl.multiple_of(which * half + first, 16), out.shape[1])
        one, two = f1[at], f[at]
        out[0] = one * w1[at].astype(F32) + two * w2[at].astype(F32)
        out[1] = one + two

    first = 0
    for send in sends:
        write(send, 1 - me, first)
        first += send.shape[1]
    write(keep, me, 0)


def share_kernel(first, keep, got, q):
    at = pl.ds(first, q.shape[0])
    den = keep[1, at] + got[1]
    q[...] = ((keep[0, at] + got[0]) / (den + EPS)).astype(BF16)


def whole_kernel(chunks, *refs):
    *parts, out, sems = refs
    lo, me, _, _ = place()
    half = sum(chunks)
    outs, first = [], 0
    for k, n in enumerate(chunks):
        spots = ((lo, me), (lo, 1 - me), (1 - lo, me), (1 - lo, 1 - me))
        for i, (l, c) in enumerate(spots):
            at = pl.ds(pl.multiple_of((2 * l + c) * half + first, 16), n)
            outs.append(pltpu.make_async_copy(parts[4 * k + i], out.at[at], sems.at[k, i]))
        first += n
    for c in outs:
        c.start()
    for c in outs:
        c.wait()


def cost(flops, moved):
    return pl.CostEstimate(flops=flops, bytes_accessed=moved, transcendentals=0)


def body(acts, grads, weights):
    _, count, tok, rows = acts.shape
    cols = grads.shape[3]
    half = rows // 2
    total = tok * 8
    lo = lax.axis_index("task") // 2
    have = {"g": [grads[0]]}

    def part(x, which, axis):
        return lax.dynamic_slice_in_dim(x, which * half, half, axis)

    def run(name, move, source, *after):
        x = have[source[0]][source[1]]
        if after:
            x = lax.optimization_barrier((x, *[have[n][i] for n, i in after]))[0]
        have.setdefault(name, []).append(move(x))

    have["o"] = [part(acts[0], lo, 2)]
    have["give"] = [part(acts[0], 1 - lo, 2)]
    have["wgive"], first = [], 0
    for n in PIECES:
        at = (1 - lo) * half + first
        have["wgive"].append(lax.dynamic_slice_in_dim(weights[0], at, n, 0))
        first += n
    for line in ORDER:
        name, source, at, *after = line.replace("<", ",").split(",")
        move = {"o": ring_z, "t": ring_z, "g": ring_y, "d": ring_y, "u": ring_y}.get(name, pair)
        if name == "x" or line.startswith("u,d"):
            move = cross
        if line.startswith(("t,give", "d,g")):
            move = pair
        run(name, move, (source, int(at)), *[(x[0], int(x[1:])) for x in after])

    grad_from = [(k, flip) for flip in (0, 1) for k in range(4)]
    sems = pltpu.SemaphoreType.DMA((count,))
    arrays = [*have["o"], *have["g"], *have["u"]]
    f1 = pl.pallas_call(
        functools.partial(first_kernel, 8, grad_from),
        out_shape=jax.ShapeDtypeStruct((half, cols), F32),
        in_specs=[HBM] * len(arrays),
        out_specs=HBM,
        scratch_shapes=[
            pltpu.VMEM((count, total, half), BF16),
            pltpu.VMEM((count, total, cols), BF16),
            pltpu.VMEM((half, cols), F32),
            sems,
            pltpu.SemaphoreType.DMA,
        ],
        compiler_params=LIMIT,
        cost_estimate=cost(2 * count * total * half * cols, 12 * 2**20),
        name="own_task",
    )(*[far(x) for x in arrays])
    arrays = [*have["t"], *have["d"], *have["x"], f1, weights, *have["w"]]
    quarter = half // 2
    keep, *sends = pl.pallas_call(
        functools.partial(second_kernel, 8, grad_from),
        out_shape=[pltpu.VMEM((2, n, cols), F32) for n in (quarter, *CHUNKS)],
        in_specs=[HBM] * len(arrays),
        out_specs=[NEAR] * (1 + len(CHUNKS)),
        scratch_shapes=[
            pltpu.VMEM((count, total, half), BF16),
            pltpu.VMEM((count, total, cols), BF16),
            pltpu.VMEM((half, cols), F32),
            pltpu.VMEM((half, cols), F32),
            pltpu.VMEM((half, cols), BF16),
            pltpu.VMEM((half, cols), BF16),
            sems,
            pltpu.SemaphoreType.DMA((2 + len(PIECES),)),
        ],
        compiler_params=LIMIT,
        cost_estimate=cost(2 * count * total * half * cols, 24 * 2**20),
        name="other_task",
    )(*[far(x) for x in arrays])
    parts, first = [], 0
    for n, send in zip(CHUNKS, sends):
        got = core(send)
        q = pl.pallas_call(
            functools.partial(share_kernel, first),
            out_shape=pltpu.VMEM((n, cols), BF16),
            in_specs=[NEAR] * 2,
            out_specs=NEAR,
            compiler_params=LITTLE,
            name="share",
        )(near(keep), near(got))
        by_pair = pair(q)
        parts += [q, core(q), by_pair, core(by_pair)]
        first += n
    return pl.pallas_call(
        functools.partial(whole_kernel, CHUNKS),
        out_shape=jax.ShapeDtypeStruct((rows, cols), BF16),
        in_specs=[NEAR] * len(parts),
        out_specs=HBM,
        scratch_shapes=[pltpu.SemaphoreType.DMA((len(CHUNKS), 4))],
        compiler_params=LITTLE,
        name="whole",
    )(*[near(p) for p in parts])


def solution(mesh):
    placed = (P("task", None, "col", "row"), P("task", None, "row", "col"), P("task", "row", "col"))
    return jax.shard_map(
        body, mesh=mesh, in_specs=placed, out_specs=P("row", "col"), check_vma=False
    )
```

```python
import functools

import jax
import jax.numpy as jnp
from jax import lax
from jax.experimental import pallas as pl
from jax.experimental.pallas import tpu as pltpu
from jax.sharding import PartitionSpec as P

EPS = 1e-06
F32, BF16 = jnp.float32, jnp.bfloat16
HBM = pl.BlockSpec(memory_space=pltpu.HBM)
NEAR = pl.BlockSpec(memory_space=pltpu.VMEM)
LIMIT = pltpu.CompilerParams(vmem_limit_bytes=36 * 2**20)
LITTLE = pltpu.CompilerParams(vmem_limit_bytes=16 * 2**20)
PIECES = (896,)
CHUNKS = (192, 256)


ORDER = (
    "o,o,0",
    "t,give,0",
    "g,g,0",
    "x,g,0",
    "o,o,1",
    "t,t,0",
    "d,g,0",
    "w,wgive,0",
    "g,g,1",
    "x,g,1",
    "o,o,2",
    "t,t,1",
    "u,d,0",
    "g,g,2",
    "d,d,0",
    "o,o,3",
    "t,t,2",
    "d,d,1",
    "u,u,0",
    "x,g,2<t1<w0",
    "o,o,4<d2",
    "t,t,3<x0<g3",
    "d,d,2",
    "u,u,1",
    "x,g,3",
    "o,o,5",
    "t,t,4",
    "u,u,2",
    "o,o,6",
    "t,t,5<x1",
    "t,t,6<x2",
)


def near(x):
    return pltpu.with_memory_space_constraint(x, pltpu.VMEM)


def far(x):
    return pltpu.with_memory_space_constraint(x, pltpu.HBM)


def place():
    task, row = lax.axis_index("task"), lax.axis_index("row")
    return task // 2, task % 2, row // 2, row % 2


def ring_y(x):
    perm = [
        (t * 8 + 2 * y + h, t * 8 + 2 * ((y + 1 - 2 * (t % 2)) % 4) + h)
        for t in range(4)
        for y in range(4)
        for h in range(2)
    ]
    return lax.ppermute(x, ("task", "row"), perm)


def ring_z(x):
    perm = [(t * 8 + z, t * 8 + (z + 1 - 2 * (t % 2)) % 8) for t in range(4) for z in range(8)]
    return lax.ppermute(x, ("task", "col"), perm)


def cross(x):
    perm = [(t * 8 + r, (t ^ 2) * 8 + (r ^ 1)) for t in range(4) for r in range(8)]
    return lax.ppermute(x, ("task", "row"), perm)


def pair(x):
    return lax.ppermute(x, "task", [(t, t ^ 2) for t in range(4)])


def core(x):
    return lax.ppermute(x, "task", [(t, t ^ 1) for t in range(4)])


def grad_block(back, flip):
    _, me, y, hi = place()
    return 2 * ((y + 4 + (2 * me - 1) * back) % 4) + (hi ^ flip if flip else hi)


def act_block(back):
    return (lax.axis_index("col") + 8 + (2 * lax.rem(lax.axis_index("task"), 2) - 1) * back) % 8


def fetch(grad_from, late, acts, grads, a, g, sems):
    count, tok = a.shape[0], a.shape[1] // 8

    def act_rows(back):
        return pl.ds(pl.multiple_of(tok * act_block(back), tok), tok)

    def grad_rows(i):
        return pl.ds(pl.multiple_of(tok * grad_block(*grad_from[i]), tok), tok)

    def begin():
        for s in range(count):
            for back, piece in enumerate(acts[:-1]):
                pltpu.make_async_copy(piece.at[s], a.at[s, act_rows(back)], sems.at[s]).start()
            for i, piece in enumerate(grads):
                if i not in late:
                    pltpu.make_async_copy(piece.at[s], g.at[s, grad_rows(i)], sems.at[s]).start()

    def arrive(s):
        some, more = a.at[s, pl.ds(0, 7 * tok)], g.at[s, pl.ds(0, (8 - len(late)) * tok)]
        pltpu.make_async_copy(some, some, sems.at[s]).wait()
        pltpu.make_async_copy(more, more, sems.at[s]).wait()
        a[s, act_rows(7)] = acts[7][s]
        for i in late:
            g[s, grad_rows(i)] = grads[i][s]

    return begin, arrive


def square_sum(arrive, count, a, g, f):
    def step(s, _):
        arrive(s)
        d = lax.dot_general(
            a[s], g[s], (((0,), (0,)), ((), ())), preferred_element_type=F32
        )
        f[...] = jnp.where(s == 0, 0.0, f[...]) + d * d
        return 0

    lax.fori_loop(0, count, step, 0)


def first_kernel(n, grad_from, late, *refs):
    m = len(grad_from)
    acts, grads, (out, a, g, sems) = refs[:n], refs[n : n + m], refs[n + m :]
    begin, arrive = fetch(grad_from, late, acts, grads, a, g, sems)
    begin()
    square_sum(arrive, a.shape[0], a, g, out)


def second_kernel(n, grad_from, late, *refs):
    m = len(grad_from)
    acts, grads = refs[:n], refs[n : n + m]
    f1, w1_hbm, *w2_hbm = refs[n + m : n + m + 2 + len(PIECES)]
    keep, *sends, a, g, f, w1, w2, sems, xsem = refs[n + m + 2 + len(PIECES) :]
    begin, arrive = fetch(grad_from, late, acts, grads, a, g, sems)
    count, size = a.shape[0], f.shape[0]
    lo, me, _, _ = place()
    half = size // 2
    own = pl.ds(pl.multiple_of(lo * size, 16), size)
    extra = [
        pltpu.make_async_copy(w1_hbm.at[0, own], w1, xsem.at[0]),
    ]
    first = 0
    for i, piece in enumerate(w2_hbm):
        at = pl.ds(first, piece.shape[0])
        extra.append(pltpu.make_async_copy(piece, w2.at[at], xsem.at[1 + i]))
        first += piece.shape[0]
    begin()
    for c in extra:
        c.start()
    square_sum(arrive, count, a, g, f)
    for c in extra:
        c.wait()

    def write(out, which, first):
        at = pl.ds(pl.multiple_of(which * half + first, 16), out.shape[1])
        one, two = f1[at], f[at]
        out[0] = one * w1[at].astype(F32) + two * w2[at].astype(F32)
        out[1] = one + two

    first = 0
    for send in sends:
        write(send, 1 - me, first)
        first += send.shape[1]
    write(keep, me, 0)


def share_kernel(first, keep, got, q):
    at = pl.ds(first, q.shape[0])
    den = keep[1, at] + got[1]
    q[...] = ((keep[0, at] + got[0]) / (den + EPS)).astype(BF16)


def whole_kernel(spots, half, *refs):
    refs = refs[-len(spots) - 2 :]
    *parts, out, sems = refs
    lo, me, _, _ = place()
    outs = []
    for i, (part, (l, c, first)) in enumerate(zip(parts, spots)):
        l, c = (1 - lo if l else lo), (1 - me if c else me)
        at = pl.ds(pl.multiple_of((2 * l + c) * half + first, 16), part.shape[0])
        outs.append(pltpu.make_async_copy(part, out.at[at], sems.at[i]))
    for c in outs:
        c.start()
    for c in outs:
        c.wait()


def cost(flops, moved):
    return pl.CostEstimate(flops=flops, bytes_accessed=moved, transcendentals=0)


def body(acts, grads, weights):
    _, count, tok, rows = acts.shape
    cols = grads.shape[3]
    half = rows // 2
    total = tok * 8
    lo = lax.axis_index("task") // 2
    have = {"g": [grads[0]]}

    def part(x, which, axis):
        return lax.dynamic_slice_in_dim(x, which * half, half, axis)

    def run(name, move, source, *after):
        x = have[source[0]][source[1]]
        if after:
            x = lax.optimization_barrier((x, *[have[n][i] for n, i in after]))[0]
        have.setdefault(name, []).append(move(x))

    have["o"] = [part(acts[0], lo, 2)]
    have["give"] = [part(acts[0], 1 - lo, 2)]
    have["wgive"], first = [], 0
    for n in PIECES:
        at = (1 - lo) * half + first
        have["wgive"].append(lax.dynamic_slice_in_dim(weights[0], at, n, 0))
        first += n
    for line in ORDER:
        name, source, at, *after = line.replace("<", ",").split(",")
        move = {"o": ring_z, "t": ring_z, "g": ring_y, "d": ring_y, "u": ring_y}.get(name, pair)
        if name == "x" or line.startswith("u,d"):
            move = cross
        if line.startswith(("t,give", "d,g")):
            move = pair
        run(name, move, (source, int(at)), *[(x[0], int(x[1:])) for x in after])

    grad_from = [(k, flip) for flip in (0, 1) for k in range(4)]
    sems = pltpu.SemaphoreType.DMA((count,))
    arrays = [*have["o"], *have["g"], *have["u"]]
    late = (7,)
    near_at = [7, *(8 + i for i in late)]
    f1 = pl.pallas_call(
        functools.partial(first_kernel, 8, grad_from, late),
        out_shape=pltpu.VMEM((half, cols), F32),
        in_specs=[NEAR if i in near_at else HBM for i in range(len(arrays))],
        out_specs=NEAR,
        scratch_shapes=[
            pltpu.VMEM((count, total, half), BF16),
            pltpu.VMEM((count, total, cols), BF16),
            sems,
        ],
        compiler_params=LIMIT,
        cost_estimate=cost(2 * count * total * half * cols, 12 * 2**20),
        name="own_task",
    )(*[near(x) if i in near_at else far(x) for i, x in enumerate(arrays)])
    arrays = [*have["t"], *have["d"], *have["x"], f1, weights, *have["w"]]
    quarter = half // 2
    late = (3, 7)
    near_at = [7, *(8 + i for i in late), 16]
    keep, *sends = pl.pallas_call(
        functools.partial(second_kernel, 8, grad_from, late),
        out_shape=[pltpu.VMEM((2, n, cols), F32) for n in (quarter, *CHUNKS)],
        in_specs=[NEAR if i in near_at else HBM for i in range(len(arrays))],
        out_specs=[NEAR] * (1 + len(CHUNKS)),
        scratch_shapes=[
            pltpu.VMEM((count, total, half), BF16),
            pltpu.VMEM((count, total, cols), BF16),
            pltpu.VMEM((half, cols), F32),
            pltpu.VMEM((half, cols), BF16),
            pltpu.VMEM((half, cols), BF16),
            sems,
            pltpu.SemaphoreType.DMA((1 + len(PIECES),)),
        ],
        compiler_params=LIMIT,
        cost_estimate=cost(2 * count * total * half * cols, 24 * 2**20),
        name="other_task",
    )(*[near(x) if i in near_at else far(x) for i, x in enumerate(arrays)])
    parts, first = [], 0
    for n, send in zip(CHUNKS, sends):
        got = core(send)
        q = pl.pallas_call(
            functools.partial(share_kernel, first),
            out_shape=pltpu.VMEM((n, cols), BF16),
            in_specs=[NEAR] * 2,
            out_specs=NEAR,
            compiler_params=LITTLE,
            name="share",
        )(near(keep), near(got))
        by_pair = pair(q)
        parts += [(q, (0, 0, first)), (core(q), (0, 1, first))]
        parts += [(by_pair, (1, 0, first)), (core(by_pair), (1, 1, first))]
        first += n
    out = None
    for some in (parts[:2] + parts[4:], parts[2:4]):
        args = [near(x) for x, _ in some]
        out = pl.pallas_call(
            functools.partial(whole_kernel, [spot for _, spot in some], quarter),
            out_shape=jax.ShapeDtypeStruct((rows, cols), BF16),
            in_specs=[HBM] * (out is not None) + [NEAR] * len(args),
            out_specs=HBM,
            scratch_shapes=[pltpu.SemaphoreType.DMA((len(args),))],
            input_output_aliases={} if out is None else {0: 0},
            compiler_params=LITTLE,
            name="whole",
        )(*([] if out is None else [out]), *args)
    return out


def solution(mesh):
    placed = (P("task", None, "col", "row"), P("task", None, "row", "col"), P("task", "row", "col"))
    return jax.shard_map(
        body, mesh=mesh, in_specs=placed, out_specs=P("row", "col"), check_vma=False
    )
```

```python
import functools

import jax
import jax.numpy as jnp
from jax import lax
from jax.experimental import pallas as pl
from jax.experimental.pallas import tpu as pltpu
from jax.sharding import PartitionSpec as P

EPS = 1e-06
F32, BF16 = jnp.float32, jnp.bfloat16
HBM = pl.BlockSpec(memory_space=pltpu.HBM)
NEAR = pl.BlockSpec(memory_space=pltpu.VMEM)
LIMIT = pltpu.CompilerParams(vmem_limit_bytes=36 * 2**20)
LITTLE = pltpu.CompilerParams(vmem_limit_bytes=16 * 2**20)
PIECES = (896,)
CHUNKS = (96, 192, 160)


ORDER = (
    "o,o,0",
    "t,give,0",
    "g,g,0",
    "x,g,0",
    "o,o,1",
    "t,t,0",
    "d,g,0",
    "w,wgive,0",
    "g,g,1",
    "x,g,1",
    "o,o,2",
    "t,t,1",
    "u,d,0",
    "g,g,2",
    "d,d,0",
    "o,o,3",
    "t,t,2",
    "d,d,1",
    "u,u,0",
    "x,g,2<t1<w0",
    "o,o,4<d2",
    "t,t,3<x0<g3",
    "d,d,2",
    "u,u,1",
    "x,g,3",
    "o,o,5",
    "t,t,4",
    "u,u,2",
    "o,o,6",
    "t,t,5<x1",
    "t,t,6<x2",
)


def near(x):
    return pltpu.with_memory_space_constraint(x, pltpu.VMEM)


def far(x):
    return pltpu.with_memory_space_constraint(x, pltpu.HBM)


def place():
    task, row = lax.axis_index("task"), lax.axis_index("row")
    return task // 2, task % 2, row // 2, row % 2


def ring_y(x):
    perm = [
        (t * 8 + 2 * y + h, t * 8 + 2 * ((y + 1 - 2 * (t % 2)) % 4) + h)
        for t in range(4)
        for y in range(4)
        for h in range(2)
    ]
    return lax.ppermute(x, ("task", "row"), perm)


def ring_z(x):
    perm = [(t * 8 + z, t * 8 + (z + 1 - 2 * (t % 2)) % 8) for t in range(4) for z in range(8)]
    return lax.ppermute(x, ("task", "col"), perm)


def cross(x):
    perm = [(t * 8 + r, (t ^ 2) * 8 + (r ^ 1)) for t in range(4) for r in range(8)]
    return lax.ppermute(x, ("task", "row"), perm)


def pair(x):
    return lax.ppermute(x, "task", [(t, t ^ 2) for t in range(4)])


def core(x):
    return lax.ppermute(x, "task", [(t, t ^ 1) for t in range(4)])


def grad_block(back, flip):
    _, me, y, hi = place()
    return 2 * ((y + 4 + (2 * me - 1) * back) % 4) + (hi ^ flip if flip else hi)


def act_block(back):
    return (lax.axis_index("col") + 8 + (2 * lax.rem(lax.axis_index("task"), 2) - 1) * back) % 8


def fetch(grad_from, late, acts, grads, a, g, sems):
    count, tok = a.shape[0], a.shape[1] // 8

    def act_rows(back):
        return pl.ds(pl.multiple_of(tok * act_block(back), tok), tok)

    def grad_rows(i):
        return pl.ds(pl.multiple_of(tok * grad_block(*grad_from[i]), tok), tok)

    def begin():
        for s in range(count):
            for back, piece in enumerate(acts[:-1]):
                pltpu.make_async_copy(piece.at[s], a.at[s, act_rows(back)], sems.at[s]).start()
            for i, piece in enumerate(grads):
                if i not in late:
                    pltpu.make_async_copy(piece.at[s], g.at[s, grad_rows(i)], sems.at[s]).start()

    def arrive(s):
        some, more = a.at[s, pl.ds(0, 7 * tok)], g.at[s, pl.ds(0, (8 - len(late)) * tok)]
        pltpu.make_async_copy(some, some, sems.at[s]).wait()
        pltpu.make_async_copy(more, more, sems.at[s]).wait()
        a[s, act_rows(7)] = acts[7][s]
        for i in late:
            g[s, grad_rows(i)] = grads[i][s]

    return begin, arrive


def square_sum(arrive, count, a, g, f):
    for s in range(count):
        arrive(s)
        d = lax.dot_general(
            a[s], g[s], (((0,), (0,)), ((), ())), preferred_element_type=F32
        )
        f[...] = d * d if s == 0 else f[...] + d * d


def first_kernel(n, grad_from, late, *refs):
    m = len(grad_from)
    acts, grads, (out, a, g, sems) = refs[:n], refs[n : n + m], refs[n + m :]
    begin, arrive = fetch(grad_from, late, acts, grads, a, g, sems)
    begin()
    square_sum(arrive, a.shape[0], a, g, out)


def second_kernel(n, grad_from, late, *refs):
    m = len(grad_from)
    acts, grads = refs[:n], refs[n : n + m]
    f1, w1_hbm, *w2_hbm = refs[n + m : n + m + 2 + len(PIECES)]
    keep, *sends, a, g, f, w1, w2, sems, xsem = refs[n + m + 2 + len(PIECES) :]
    begin, arrive = fetch(grad_from, late, acts, grads, a, g, sems)
    count, size = a.shape[0], f.shape[0]
    lo, me, _, _ = place()
    half = size // 2
    own = pl.ds(pl.multiple_of(lo * size, 16), size)
    extra = [
        pltpu.make_async_copy(w1_hbm.at[0, own], w1, xsem.at[0]),
    ]
    first = 0
    for i, piece in enumerate(w2_hbm):
        at = pl.ds(first, piece.shape[0])
        extra.append(pltpu.make_async_copy(piece, w2.at[at], xsem.at[1 + i]))
        first += piece.shape[0]
    begin()
    for c in extra:
        c.start()
    square_sum(arrive, count, a, g, f)
    for c in extra:
        c.wait()

    def write(out, which, first):
        at = pl.ds(pl.multiple_of(which * half + first, 16), out.shape[1])
        one, two = f1[at], f[at]
        out[0] = one * w1[at].astype(F32) + two * w2[at].astype(F32)
        out[1] = one + two

    first = 0
    for send in sends:
        write(send, 1 - me, first)
        first += send.shape[1]
    write(keep, me, 0)


def share_kernel(first, keep, got, q):
    at = pl.ds(first, q.shape[0])
    den = keep[1, at] + got[1]
    q[...] = ((keep[0, at] + got[0]) / (den + EPS)).astype(BF16)


def whole_kernel(spots, half, *refs):
    refs = refs[-len(spots) - 2 :]
    *parts, out, sems = refs
    lo, me, _, _ = place()
    outs = []
    for i, (part, (l, c, first)) in enumerate(zip(parts, spots)):
        l, c = (1 - lo if l else lo), (1 - me if c else me)
        at = pl.ds(pl.multiple_of((2 * l + c) * half + first, 16), part.shape[0])
        outs.append(pltpu.make_async_copy(part, out.at[at], sems.at[i]))
    for c in outs:
        c.start()
    for c in outs:
        c.wait()


def cost(flops, moved):
    return pl.CostEstimate(flops=flops, bytes_accessed=moved, transcendentals=0)


def body(acts, grads, weights):
    _, count, tok, rows = acts.shape
    cols = grads.shape[3]
    half = rows // 2
    total = tok * 8
    lo = lax.axis_index("task") // 2
    have = {"g": [grads[0]]}

    def part(x, which, axis):
        return lax.dynamic_slice_in_dim(x, which * half, half, axis)

    def run(name, move, source, *after):
        x = have[source[0]][source[1]]
        if after:
            x = lax.optimization_barrier((x, *[have[n][i] for n, i in after]))[0]
        have.setdefault(name, []).append(move(x))

    have["o"] = [part(acts[0], lo, 2)]
    have["give"] = [part(acts[0], 1 - lo, 2)]
    have["wgive"], first = [], 0
    for n in PIECES:
        at = (1 - lo) * half + first
        have["wgive"].append(lax.dynamic_slice_in_dim(weights[0], at, n, 0))
        first += n
    for line in ORDER:
        name, source, at, *after = line.replace("<", ",").split(",")
        move = {"o": ring_z, "t": ring_z, "g": ring_y, "d": ring_y, "u": ring_y}.get(name, pair)
        if name == "x" or line.startswith("u,d"):
            move = cross
        if line.startswith(("t,give", "d,g")):
            move = pair
        run(name, move, (source, int(at)), *[(x[0], int(x[1:])) for x in after])

    grad_from = [(k, flip) for flip in (0, 1) for k in range(4)]
    sems = pltpu.SemaphoreType.DMA((count,))
    arrays = [*have["o"], *have["g"], *have["u"]]
    late = (7,)
    near_at = [7, *(8 + i for i in late)]
    f1 = pl.pallas_call(
        functools.partial(first_kernel, 8, grad_from, late),
        out_shape=pltpu.VMEM((half, cols), F32),
        in_specs=[NEAR if i in near_at else HBM for i in range(len(arrays))],
        out_specs=NEAR,
        scratch_shapes=[
            pltpu.VMEM((count, total, half), BF16),
            pltpu.VMEM((count, total, cols), BF16),
            sems,
        ],
        compiler_params=LIMIT,
        cost_estimate=cost(2 * count * total * half * cols, 12 * 2**20),
        name="own_task",
    )(*[near(x) if i in near_at else far(x) for i, x in enumerate(arrays)])
    arrays = [*have["t"], *have["d"], *have["x"], f1, weights, *have["w"]]
    quarter = half // 2
    late = (3, 7)
    near_at = [7, *(8 + i for i in late), 16]
    keep, *sends = pl.pallas_call(
        functools.partial(second_kernel, 8, grad_from, late),
        out_shape=[pltpu.VMEM((2, n, cols), F32) for n in (quarter, *CHUNKS)],
        in_specs=[NEAR if i in near_at else HBM for i in range(len(arrays))],
        out_specs=[NEAR] * (1 + len(CHUNKS)),
        scratch_shapes=[
            pltpu.VMEM((count, total, half), BF16),
            pltpu.VMEM((count, total, cols), BF16),
            pltpu.VMEM((half, cols), F32),
            pltpu.VMEM((half, cols), BF16),
            pltpu.VMEM((half, cols), BF16),
            sems,
            pltpu.SemaphoreType.DMA((1 + len(PIECES),)),
        ],
        compiler_params=LIMIT,
        cost_estimate=cost(2 * count * total * half * cols, 24 * 2**20),
        name="other_task",
    )(*[near(x) if i in near_at else far(x) for i, x in enumerate(arrays)])
    parts, first = [], 0
    for n, send in zip(CHUNKS, sends):
        got = core(send)
        q = pl.pallas_call(
            functools.partial(share_kernel, first),
            out_shape=pltpu.VMEM((n, cols), BF16),
            in_specs=[NEAR] * 2,
            out_specs=NEAR,
            compiler_params=LITTLE,
            name="share",
        )(near(keep), near(got))
        by_pair = pair(q)
        parts += [(q, (0, 0, first)), (core(q), (0, 1, first))]
        parts += [(by_pair, (1, 0, first)), (core(by_pair), (1, 1, first))]
        first += n
    out = None
    for some in (parts[:2] + parts[4:], parts[2:4]):
        args = [near(x) for x, _ in some]
        out = pl.pallas_call(
            functools.partial(whole_kernel, [spot for _, spot in some], quarter),
            out_shape=jax.ShapeDtypeStruct((rows, cols), BF16),
            in_specs=[HBM] * (out is not None) + [NEAR] * len(args),
            out_specs=HBM,
            scratch_shapes=[pltpu.SemaphoreType.DMA((len(args),))],
            input_output_aliases={} if out is None else {0: 0},
            compiler_params=LITTLE,
            name="whole",
        )(*([] if out is None else [out]), *args)
    return out


def solution(mesh):
    placed = (P("task", None, "col", "row"), P("task", None, "row", "col"), P("task", "row", "col"))
    return jax.shard_map(
        body, mesh=mesh, in_specs=placed, out_specs=P("row", "col"), check_vma=False
    )
```
